32 devices in a mesh: psg: 8 (over z, x), cen: 4 (over y, core).
Axes of the slice: x: 2, y: 2, z: 4, core: 2. Of those that a mesh axis runs over, the one named last changes fastest.
Arguments:
- passages: bfloat16 [256, 4096], P('psg'), may hold values from -8 to 8
- centroids: bfloat16 [65536, 4096], P(('psg', 'cen')), may hold values from -4 to 4
- dual_init: float32 [65536], P(('psg', 'cen')), may hold values from -8 to 8
Outputs:
- new_centroids: bfloat16 [65536, 4096], P(('psg', 'cen'))
- passage_duals: float32 [256], P('psg')
- centroid_duals: float32 [65536], P(('psg', 'cen'))
The draws below stay inside these ranges and needn't reach their ends.
All inputs are finite; a program needn't handle non-finite values.
Results may differ from the reference program's by a relative error of at most 0.0047.
Values may be sent and summed in bfloat16 or wider, within the bound.
A program may use at most 64 MiB of HBM per device.

```python
import math
import jax
import jax.numpy as jnp

D = 4096
CENTROIDS = 65536
ITERS = 3
PASSAGES = 256


def centroid_table(key):
    table = jax.random.normal(key, (CENTROIDS, D), jnp.float32)
    return jnp.clip(table, -4.0, 4.0)


def draw_centroids(key, part):
    table = centroid_table(key)
    return table.astype(jnp.bfloat16)


def draw_passages(key, part):
    key = jax.random.fold_in(key, 3)
    values = jnp.clip(jax.random.normal(key, (PASSAGES, D), jnp.float32), -6.0, 6.0)
    return jnp.clip(values, -8.0, 8.0).astype(jnp.bfloat16)


def steps_of(rng, extent, shards, smallest, high):
    factor_of = 1.0
    for axis_at, blocks in shards:
        draws = jax.random.uniform(jax.random.fold_in(jax.random.fold_in(rng, 6), axis_at), (blocks,), jnp.float32, smallest / len(shards), high / len(shards))
        factor_of = factor_of * jnp.repeat(jnp.exp(draws), extent[axis_at] // blocks).reshape((-1,) + (1,) * (len(extent) - 1 - axis_at))
    return factor_of


def gaussian(own_key, shape, scale, limit, shards=(), held_as=jnp.bfloat16):
    entries = jax.random.normal(own_key, shape, jnp.float32) * scale
    if len(shards) > 0:
        entries = steps_of(own_key, shape, shards, -0.22, 0.18) * entries
    return jnp.clip(entries, min=-limit, max=limit).astype(held_as)


def setup_inputs(seed: int = 0) -> dict:
    splits = jax.random.split(jax.random.key(seed), 4)
    return {
        "passages": draw_passages(jax.random.fold_in(splits[3], 71), 0),
        "centroids": draw_centroids(jax.random.fold_in(splits[3], 71), 0),
        "dual_init": gaussian(splits[2], (CENTROIDS,), 2.0, 8.0, ((0, 32),), jnp.float32),
    }


def reference(passages, centroids, dual_init):
    factor = 4.0 / math.sqrt(D)
    logits = jnp.dot(passages, centroids.T, preferred_element_type=jnp.float32) * factor
    centroid_duals = dual_init
    passage_duals = jnp.zeros((PASSAGES,), jnp.float32)
    for number in range(ITERS):
        passage_duals = -math.log(PASSAGES) - jax.nn.logsumexp(logits + centroid_duals[None, :], axis=1)
        centroid_duals = -math.log(CENTROIDS) - jax.nn.logsumexp(logits + passage_duals[:, None], axis=0)
    weight = (CENTROIDS * jnp.exp(logits + passage_duals[:, None] + centroid_duals[None, :])).astype(jnp.bfloat16)
    new_centroids = jnp.dot(weight.T, passages, preferred_element_type=jnp.float32).astype(jnp.bfloat16)
    return (new_centroids, passage_duals, centroid_duals)
```

```python
import functools
import math

import jax
import jax.numpy as jnp
from jax import lax
from jax.experimental import pallas as pl
from jax.experimental.pallas import tpu as pltpu
from jax.sharding import PartitionSpec as P

CENTROIDS = 65536
ITERS = 3
LANES = 128
MESH = pl.DeviceIdType.MESH


def kernel(
    n_psg, n_cen,
    rows_ref, table_ref, init_ref,
    weight_ref, gathered_out, duals_ref, cen_duals_ref,
    table, gathered, logits, lane_top, lane_sum, duals_wide, cen_buf, psg_buf,
    table_sem, own_sem, spread_send, spread_recv, pass_send, pass_recv,
    cen_send, cen_recv, psg_send, psg_recv, out_sem,
):
    me_p, me_c = lax.axis_index("psg"), lax.axis_index("cen")
    local, depth = rows_ref.shape
    count, width = logits.shape
    part = depth // n_cen
    factor = 4.0 / math.sqrt(depth)
    sibling = me_c + 1 - 2 * lax.rem(me_c, 2)
    across = lax.rem(me_c + 2, n_cen)
    diagonal = lax.rem(sibling + 2, n_cen)
    order = (me_c, sibling, across, diagonal)

    def block(index):
        return pl.ds(pl.multiple_of(index * local, local), local)

    def quarter(index):
        return pl.ds(pl.multiple_of(index * part, part), part)

    def lanes(index):
        return pl.ds(pl.multiple_of(index * LANES, LANES), LANES)

    table_copies = []
    for at, which in enumerate(order):
        copy = pltpu.make_async_copy(
            table_ref.at[:, quarter(which)], table.at[:, quarter(which)], table_sem.at[at]
        )
        copy.start()
        table_copies.append(copy)
    own = pltpu.make_async_copy(rows_ref, gathered.at[block(me_p), :], own_sem)
    own.start()

    barrier = pltpu.get_barrier_semaphore()
    for step in range(1, n_psg):
        pl.semaphore_signal(
            barrier, inc=1, device_id=(lax.rem(me_p + step, n_psg), me_c), device_id_type=MESH
        )
    for step in range(1, n_cen):
        pl.semaphore_signal(
            barrier, inc=1, device_id=(me_p, lax.rem(me_c + step, n_cen)), device_id_type=MESH
        )
    pl.semaphore_wait(barrier, n_psg + n_cen - 2)

    def remote(src, dst, send, recv, to_p, to_c):
        return pltpu.make_async_remote_copy(
            src_ref=src, dst_ref=dst, send_sem=send, recv_sem=recv,
            device_id=(to_p, to_c), device_id_type=MESH,
        )

    sent = []
    spread = [None]
    for step in range(1, n_psg):
        copy = remote(
            rows_ref.at[:, quarter(me_c)], gathered.at[block(me_p), quarter(me_c)],
            spread_send.at[step], spread_recv.at[step], lax.rem(me_p + step, n_psg), me_c,
        )
        copy.start()
        spread.append(copy)
        sent.append(copy)

    def forward(step, kind, which, to_c):
        place = gathered.at[block(lax.rem(me_p - step + n_psg, n_psg)), quarter(which)]
        copy = remote(
            place, place, pass_send.at[kind, step], pass_recv.at[kind, step], me_p, to_c
        )
        copy.start()
        sent.append(copy)
        return copy

    from_sibling, from_across, from_diagonal = [None], [None], [None]
    for step in range(1, n_psg):
        spread[step].wait_recv()
        from_across.append(forward(step, 0, me_c, across))
        from_sibling.append(forward(step, 1, me_c, sibling))
        if step >= 2:
            from_across[step - 1].wait_recv()
            from_diagonal.append(forward(step - 1, 2, across, sibling))
    from_across[n_psg - 1].wait_recv()
    from_diagonal.append(forward(n_psg - 1, 2, across, sibling))

    own.wait()
    tile = min(width, 256)
    for at, which in enumerate(order):
        arrivals = ((), from_sibling[1:], (), from_diagonal[1:])[at]
        for copy in arrivals:
            copy.wait_recv()
        table_copies[at].wait()

        def multiply(number, carry, at=at, which=which):
            columns = pl.ds(pl.multiple_of(number * tile, tile), tile)
            product = lax.dot_general(
                gathered[:, quarter(which)], table[columns, quarter(which)],
                (((1,), (1,)), ((), ())), preferred_element_type=jnp.float32,
            )
            if at > 0:
                product = logits[:, columns] + product
            if at == len(order) - 1:
                product = product * factor
            logits[:, columns] = product
            return carry

        lax.fori_loop(0, width // tile, multiply, 0)
    out_copy = pltpu.make_async_copy(gathered, gathered_out, out_sem)
    out_copy.start()

    chunks = width // LANES

    def total_rows(number):
        lane_sum[...] = jnp.zeros_like(lane_sum)

        def add(chunk, carry):
            shifted = logits[:, lanes(chunk)] + cen_duals_ref[:, lanes(chunk)]
            lane_sum[...] += jnp.exp(shifted - lane_top[...])
            return carry

        lax.fori_loop(0, chunks, add, 0, unroll=2)
        tops, sums = lane_top[...].T, lane_sum[...].T
        top = jnp.max(tops, axis=0, keepdims=True)
        total = jnp.sum(sums * jnp.exp(tops - top), axis=0, keepdims=True)
        top, total = exchange(
            number, top, total, cen_buf, cen_send, cen_recv, n_cen, me_c,
            lambda step: (me_p, lax.rem(me_c + step, n_cen)),
        )
        return exchange(
            number, top, total, psg_buf, psg_send, psg_recv, n_psg, me_p,
            lambda step: (lax.rem(me_p + step, n_psg), me_c),
        )

    def exchange(number, top, total, buf, send, recv, size, me, target):
        upper = lax.broadcasted_iota(jnp.int32, (8, count), 0) < 4
        buf[number, me] = jnp.where(upper, top, total)
        copies = []
        for step in range(1, size):
            to_p, to_c = target(step)
            copy = remote(
                buf.at[number, me], buf.at[number, me],
                send.at[number, step], recv.at[number, step], to_p, to_c,
            )
            copy.start()
            copies.append(copy)
            sent.append(copy)
        for copy in copies:
            copy.wait_recv()
        tops = [buf[number, other, 0:1, :] for other in range(size)]
        sums = [buf[number, other, 4:5, :] for other in range(size)]
        top = functools.reduce(jnp.maximum, tops)
        total = functools.reduce(
            jnp.add, [value * jnp.exp(high - top) for high, value in zip(tops, sums)]
        )
        return top, total

    cen_duals_ref[...] = init_ref[...]
    lane_top[...] = jnp.full_like(lane_top, -jnp.inf)

    def first_top(chunk, carry):
        lane_top[...] = jnp.maximum(
            lane_top[...], logits[:, lanes(chunk)] + init_ref[:, lanes(chunk)]
        )
        return carry

    lax.fori_loop(0, chunks, first_top, 0, unroll=2)

    for number in range(ITERS):
        top, total = total_rows(number)
        duals = -math.log(count) - (top + jnp.log(total))
        duals_wide[...] = jnp.broadcast_to(duals, (LANES, count)).T
        last = number == ITERS - 1
        if last:
            duals_ref[...] = duals
        else:
            lane_top[...] = jnp.full_like(lane_top, -jnp.inf)

        def columns_pass(chunk, carry, last=last):
            terms = logits[:, lanes(chunk)] + duals_wide[...]
            column_top = jnp.max(terms, axis=0, keepdims=True)
            column_sum = jnp.sum(jnp.exp(terms - column_top), axis=0, keepdims=True)
            fresh = -math.log(CENTROIDS) - (column_top + jnp.log(column_sum))
            cen_duals_ref[:, lanes(chunk)] = fresh
            if last:
                weight_ref[:, lanes(chunk)] = (CENTROIDS * jnp.exp(terms + fresh)).astype(
                    jnp.bfloat16
                )
            else:
                lane_top[...] = jnp.maximum(lane_top[...], logits[:, lanes(chunk)] + fresh)
            return carry

        lax.fori_loop(0, chunks, columns_pass, 0, unroll=2)

    for copy in sent:
        copy.wait_send()
    out_copy.wait()


def body(n_psg, n_cen, passages, centroids, dual_init):
    local, depth = passages.shape
    width = centroids.shape[0]
    count = local * n_psg
    vmem = pl.BlockSpec(memory_space=pltpu.VMEM)
    anywhere = pl.BlockSpec(memory_space=pl.ANY)
    dma = pltpu.SemaphoreType.DMA
    weight, gathered, passage_duals, centroid_duals = pl.pallas_call(
        functools.partial(kernel, n_psg, n_cen),
        out_shape=(
            jax.ShapeDtypeStruct((count, width), jnp.bfloat16),
            jax.ShapeDtypeStruct((count, depth), jnp.bfloat16),
            jax.ShapeDtypeStruct((1, count), jnp.float32),
            jax.ShapeDtypeStruct((1, width), jnp.float32),
        ),
        in_specs=[vmem, anywhere, vmem],
        out_specs=(vmem, anywhere, vmem, vmem),
        scratch_shapes=[
            pltpu.VMEM((width, depth), jnp.bfloat16),
            pltpu.VMEM((count, depth), jnp.bfloat16),
            pltpu.VMEM((count, width), jnp.float32),
            pltpu.VMEM((count, LANES), jnp.float32),
            pltpu.VMEM((count, LANES), jnp.float32),
            pltpu.VMEM((count, LANES), jnp.float32),
            pltpu.VMEM((ITERS, n_cen, 8, count), jnp.float32),
            pltpu.VMEM((ITERS, n_psg, 8, count), jnp.float32),
            dma((n_cen,)),
            dma,
            dma((n_psg,)),
            dma((n_psg,)),
            dma((3, n_psg)),
            dma((3, n_psg)),
            dma((ITERS, n_cen)),
            dma((ITERS, n_cen)),
            dma((ITERS, n_psg)),
            dma((ITERS, n_psg)),
            dma,
        ],
        compiler_params=pltpu.CompilerParams(
            collective_id=0, has_side_effects=True, vmem_limit_bytes=56 * 1024 * 1024
        ),
    )(passages, centroids, dual_init.reshape(1, width))
    summed = lax.dot_general(
        weight, gathered, (((0,), (0,)), ((), ())), preferred_element_type=jnp.float32
    )
    own_duals = lax.dynamic_slice_in_dim(
        passage_duals.reshape(count), lax.axis_index("psg") * local, local
    )
    return (summed.astype(jnp.bfloat16), own_duals, centroid_duals.reshape(width))


def solution(mesh):
    in_specs = (P("psg", None), P(("psg", "cen"), None), P(("psg", "cen")))
    out_specs = (P(("psg", "cen"), None), P("psg"), P(("psg", "cen")))
    return jax.shard_map(
        functools.partial(body, mesh.shape["psg"], mesh.shape["cen"]),
        mesh=mesh, in_specs=in_specs, out_specs=out_specs, check_vma=False,
    )
```

```python
import functools
import math

import jax
import jax.numpy as jnp
from jax import lax
from jax.experimental import pallas as pl
from jax.experimental.pallas import tpu as pltpu
from jax.sharding import PartitionSpec as P

CENTROIDS = 65536
ITERS = 3
LANES = 128
MESH = pl.DeviceIdType.MESH


def kernel(
    n_psg, n_cen,
    rows_ref, table_ref, init_ref,
    weight_ref, gathered_out, duals_ref, cen_duals_ref,
    table, gathered, logits, lane_top, lane_sum, duals_wide, cen_buf, psg_buf,
    table_sem, own_sem, spread_send, spread_recv, pass_send, pass_recv,
    cen_send, cen_recv, psg_send, psg_recv, out_sem,
):
    me_p, me_c = lax.axis_index("psg"), lax.axis_index("cen")
    local, depth = rows_ref.shape
    count, width = logits.shape
    part = depth // n_cen
    factor = 4.0 / math.sqrt(depth)
    sibling = me_c + 1 - 2 * lax.rem(me_c, 2)
    across = lax.rem(me_c + 2, n_cen)
    diagonal = lax.rem(sibling + 2, n_cen)
    order = (me_c, sibling, across, diagonal)

    def block(index):
        return pl.ds(pl.multiple_of(index * local, local), local)

    def quarter(index):
        return pl.ds(pl.multiple_of(index * part, part), part)

    def lanes(index):
        return pl.ds(pl.multiple_of(index * LANES, LANES), LANES)

    table_copies = []
    for at, which in enumerate(order):
        copy = pltpu.make_async_copy(
            table_ref.at[:, quarter(which)], table.at[:, quarter(which)], table_sem.at[at]
        )
        copy.start()
        table_copies.append(copy)
    own = pltpu.make_async_copy(rows_ref, gathered.at[block(me_p), :], own_sem)
    own.start()

    barrier = pltpu.get_barrier_semaphore()
    for step in range(1, n_psg):
        pl.semaphore_signal(
            barrier, inc=1, device_id=(lax.rem(me_p + step, n_psg), me_c), device_id_type=MESH
        )
    for step in range(1, n_cen):
        pl.semaphore_signal(
            barrier, inc=1, device_id=(me_p, lax.rem(me_c + step, n_cen)), device_id_type=MESH
        )
    pl.semaphore_wait(barrier, n_psg + n_cen - 2)

    def remote(src, dst, send, recv, to_p, to_c):
        return pltpu.make_async_remote_copy(
            src_ref=src, dst_ref=dst, send_sem=send, recv_sem=recv,
            device_id=(to_p, to_c), device_id_type=MESH,
        )

    sent = []
    spread = [None]
    for step in range(1, n_psg):
        copy = remote(
            rows_ref.at[:, quarter(me_c)], gathered.at[block(me_p), quarter(me_c)],
            spread_send.at[step], spread_recv.at[step], lax.rem(me_p + step, n_psg), me_c,
        )
        copy.start()
        spread.append(copy)
        sent.append(copy)

    def forward(step, kind, which, to_c):
        place = gathered.at[block(lax.rem(me_p - step + n_psg, n_psg)), quarter(which)]
        copy = remote(
            place, place, pass_send.at[kind, step], pass_recv.at[kind, step], me_p, to_c
        )
        copy.start()
        sent.append(copy)
        return copy

    from_sibling, from_across = [], []
    for step in range(1, n_psg):
        spread[step].wait_recv()
        from_across.append(forward(step, 0, me_c, across))
        from_sibling.append(forward(step, 1, me_c, sibling))

    own.wait()
    tile = min(width, 256)

    def accumulate(at, arrivals):
        for copy in arrivals:
            copy.wait_recv()
        table_copies[at].wait()
        which = order[at]

        def multiply(number, carry):
            columns = pl.ds(pl.multiple_of(number * tile, tile), tile)
            product = lax.dot_general(
                gathered[:, quarter(which)], table[columns, quarter(which)],
                (((1,), (1,)), ((), ())), preferred_element_type=jnp.float32,
            )
            if at > 0:
                product = logits[:, columns] + product
            if at == len(order) - 1:
                product = product * factor
            logits[:, columns] = product
            return carry

        lax.fori_loop(0, width // tile, multiply, 0)

    accumulate(0, ())
    from_diagonal = []
    for step in range(1, n_psg):
        from_across[step - 1].wait_recv()
        from_diagonal.append(forward(step, 2, across, sibling))
    accumulate(1, from_sibling)
    accumulate(2, ())
    accumulate(3, from_diagonal)
    out_copy = pltpu.make_async_copy(gathered, gathered_out, out_sem)
    out_copy.start()

    chunks = width // LANES

    def total_rows(number):
        lane_sum[...] = jnp.zeros_like(lane_sum)

        def add(chunk, carry):
            shifted = logits[:, lanes(chunk)] + cen_duals_ref[:, lanes(chunk)]
            lane_sum[...] += jnp.exp(shifted - lane_top[...])
            return carry

        lax.fori_loop(0, chunks, add, 0, unroll=2)
        tops, sums = lane_top[...].T, lane_sum[...].T
        top = jnp.max(tops, axis=0, keepdims=True)
        total = jnp.sum(sums * jnp.exp(tops - top), axis=0, keepdims=True)
        top, total = exchange(
            number, top, total, cen_buf, cen_send, cen_recv, n_cen, me_c,
            lambda step: (me_p, lax.rem(me_c + step, n_cen)),
        )
        return exchange(
            number, top, total, psg_buf, psg_send, psg_recv, n_psg, me_p,
            lambda step: (lax.rem(me_p + step, n_psg), me_c),
        )

    def exchange(number, top, total, buf, send, recv, size, me, target):
        upper = lax.broadcasted_iota(jnp.int32, (8, count), 0) < 4
        buf[number, me] = jnp.where(upper, top, total)
        copies = []
        for step in range(1, size):
            to_p, to_c = target(step)
            copy = remote(
                buf.at[number, me], buf.at[number, me],
                send.at[number, step], recv.at[number, step], to_p, to_c,
            )
            copy.start()
            copies.append(copy)
            sent.append(copy)
        for copy in copies:
            copy.wait_recv()
        tops = [buf[number, other, 0:1, :] for other in range(size)]
        sums = [buf[number, other, 4:5, :] for other in range(size)]
        top = functools.reduce(jnp.maximum, tops)
        total = functools.reduce(
            jnp.add, [value * jnp.exp(high - top) for high, value in zip(tops, sums)]
        )
        return top, total

    cen_duals_ref[...] = init_ref[...]
    lane_top[...] = jnp.full_like(lane_top, -jnp.inf)

    def first_top(chunk, carry):
        lane_top[...] = jnp.maximum(
            lane_top[...], logits[:, lanes(chunk)] + init_ref[:, lanes(chunk)]
        )
        return carry

    lax.fori_loop(0, chunks, first_top, 0, unroll=2)

    for number in range(ITERS):
        top, total = total_rows(number)
        duals = -math.log(count) - (top + jnp.log(total))
        duals_wide[...] = jnp.broadcast_to(duals, (LANES, count)).T
        last = number == ITERS - 1
        if last:
            duals_ref[...] = duals
        else:
            lane_top[...] = jnp.full_like(lane_top, -jnp.inf)

        def columns_pass(chunk, carry, last=last):
            terms = logits[:, lanes(chunk)] + duals_wide[...]
            column_top = jnp.max(terms, axis=0, keepdims=True)
            column_sum = jnp.sum(jnp.exp(terms - column_top), axis=0, keepdims=True)
            fresh = -math.log(CENTROIDS) - (column_top + jnp.log(column_sum))
            cen_duals_ref[:, lanes(chunk)] = fresh
            if last:
                weight_ref[:, lanes(chunk)] = (CENTROIDS * jnp.exp(terms + fresh)).astype(
                    jnp.bfloat16
                )
            else:
                lane_top[...] = jnp.maximum(lane_top[...], logits[:, lanes(chunk)] + fresh)
            return carry

        lax.fori_loop(0, chunks, columns_pass, 0, unroll=2)

    for copy in sent:
        copy.wait_send()
    out_copy.wait()


def update_kernel(n_psg, weight_ref, gathered_ref, duals_ref, cen_ref, out_ref, own_ref, cen_out_ref):
    depth = out_ref.shape[1]
    local = own_ref.shape[1]
    step = min(depth, 512)

    @pl.when(pl.program_id(0) == 0)
    def _():
        me = lax.axis_index("psg")
        own = duals_ref[:, 0:local]
        for index in range(1, n_psg):
            own = jnp.where(me == index, duals_ref[:, index * local:(index + 1) * local], own)
        own_ref[...] = own
        cen_out_ref[...] = cen_ref[...]

    weight = weight_ref[...]
    for start in range(0, depth, step):
        out_ref[:, start:start + step] = lax.dot_general(
            weight, gathered_ref[:, start:start + step], (((0,), (0,)), ((), ())),
            preferred_element_type=jnp.float32,
        ).astype(out_ref.dtype)


def body(n_psg, n_cen, passages, centroids, dual_init):
    local, depth = passages.shape
    width = centroids.shape[0]
    count = local * n_psg
    vmem = pl.BlockSpec(memory_space=pltpu.VMEM)
    anywhere = pl.BlockSpec(memory_space=pl.ANY)
    dma = pltpu.SemaphoreType.DMA
    weight, gathered, passage_duals, centroid_duals = pl.pallas_call(
        functools.partial(kernel, n_psg, n_cen),
        out_shape=(
            jax.ShapeDtypeStruct((count, width), jnp.bfloat16),
            jax.ShapeDtypeStruct((count, depth), jnp.bfloat16),
            jax.ShapeDtypeStruct((1, count), jnp.float32),
            jax.ShapeDtypeStruct((1, width), jnp.float32),
        ),
        in_specs=[vmem, anywhere, vmem],
        out_specs=(vmem, anywhere, vmem, vmem),
        scratch_shapes=[
            pltpu.VMEM((width, depth), jnp.bfloat16),
            pltpu.VMEM((count, depth), jnp.bfloat16),
            pltpu.VMEM((count, width), jnp.float32),
            pltpu.VMEM((count, LANES), jnp.float32),
            pltpu.VMEM((count, LANES), jnp.float32),
            pltpu.VMEM((count, LANES), jnp.float32),
            pltpu.VMEM((ITERS, n_cen, 8, count), jnp.float32),
            pltpu.VMEM((ITERS, n_psg, 8, count), jnp.float32),
            dma((n_cen,)),
            dma,
            dma((n_psg,)),
            dma((n_psg,)),
            dma((3, n_psg)),
            dma((3, n_psg)),
            dma((ITERS, n_cen)),
            dma((ITERS, n_cen)),
            dma((ITERS, n_psg)),
            dma((ITERS, n_psg)),
            dma,
        ],
        compiler_params=pltpu.CompilerParams(
            collective_id=0, has_side_effects=True, vmem_limit_bytes=56 * 1024 * 1024
        ),
    )(passages, centroids, dual_init.reshape(1, width))
    tile = min(width, 256)
    new_centroids, own_duals, final_duals = pl.pallas_call(
        functools.partial(update_kernel, n_psg),
        grid=(width // tile,),
        out_shape=(
            jax.ShapeDtypeStruct((width, depth), jnp.bfloat16),
            jax.ShapeDtypeStruct((1, local), jnp.float32),
            jax.ShapeDtypeStruct((1, width), jnp.float32),
        ),
        in_specs=[
            pl.BlockSpec((count, tile), lambda i: (0, i)),
            pl.BlockSpec((count, depth), lambda i: (0, 0)),
            pl.BlockSpec((1, count), lambda i: (0, 0)),
            pl.BlockSpec((1, width), lambda i: (0, 0)),
        ],
        out_specs=(
            pl.BlockSpec((tile, depth), lambda i: (i, 0)),
            pl.BlockSpec((1, local), lambda i: (0, 0)),
            pl.BlockSpec((1, width), lambda i: (0, 0)),
        ),
        compiler_params=pltpu.CompilerParams(vmem_limit_bytes=60 * 1024 * 1024),
    )(weight, gathered, passage_duals, centroid_duals)
    return (new_centroids, own_duals.reshape(local), final_duals.reshape(width))


def solution(mesh):
    in_specs = (P("psg", None), P(("psg", "cen"), None), P(("psg", "cen")))
    out_specs = (P(("psg", "cen"), None), P("psg"), P(("psg", "cen")))
    return jax.shard_map(
        functools.partial(body, mesh.shape["psg"], mesh.shape["cen"]),
        mesh=mesh, in_specs=in_specs, out_specs=out_specs, check_vma=False,
    )
```

```python
import functools
import math

import jax
import jax.numpy as jnp
from jax import lax
from jax.experimental import pallas as pl
from jax.experimental.pallas import tpu as pltpu
from jax.sharding import PartitionSpec as P

CENTROIDS = 65536
ITERS = 3
LANES = 128
MESH = pl.DeviceIdType.MESH


def kernel(
    n_psg, n_cen,
    rows_ref, table_ref, init_ref,
    weight_ref, gathered_out, duals_ref, cen_duals_ref,
    table, gathered, logits, lane_top, lane_sum, duals_wide, cen_buf, psg_buf,
    table_sem, own_sem, spread_send, spread_recv, pass_send, pass_recv,
    cen_send, cen_recv, psg_send, psg_recv, out_sem,
):
    me_p, me_c = lax.axis_index("psg"), lax.axis_index("cen")
    local, depth = rows_ref.shape
    count, width = logits.shape
    part = depth // n_cen
    factor = 4.0 / math.sqrt(depth)
    sibling = me_c + 1 - 2 * lax.rem(me_c, 2)
    across = lax.rem(me_c + 2, n_cen)
    diagonal = lax.rem(sibling + 2, n_cen)
    order = (me_c, sibling, across, diagonal)

    def block(index):
        return pl.ds(pl.multiple_of(index * local, local), local)

    def quarter(index):
        return pl.ds(pl.multiple_of(index * part, part), part)

    def lanes(index):
        return pl.ds(pl.multiple_of(index * LANES, LANES), LANES)

    table_copies = []
    for at, which in enumerate(order):
        copy = pltpu.make_async_copy(
            table_ref.at[:, quarter(which)], table.at[:, quarter(which)], table_sem.at[at]
        )
        copy.start()
        table_copies.append(copy)
    own = pltpu.make_async_copy(rows_ref, gathered.at[block(me_p), :], own_sem)
    own.start()

    barrier = pltpu.get_barrier_semaphore()
    for step in range(1, n_psg):
        pl.semaphore_signal(
            barrier, inc=1, device_id=(lax.rem(me_p + step, n_psg), me_c), device_id_type=MESH
        )
    for step in range(1, n_cen):
        pl.semaphore_signal(
            barrier, inc=1, device_id=(me_p, lax.rem(me_c + step, n_cen)), device_id_type=MESH
        )
    pl.semaphore_wait(barrier, n_psg + n_cen - 2)

    def remote(src, dst, send, recv, to_p, to_c):
        return pltpu.make_async_remote_copy(
            src_ref=src, dst_ref=dst, send_sem=send, recv_sem=recv,
            device_id=(to_p, to_c), device_id_type=MESH,
        )

    sent = []
    spread = [None]
    for step in range(1, n_psg):
        copy = remote(
            rows_ref.at[:, quarter(me_c)], gathered.at[block(me_p), quarter(me_c)],
            spread_send.at[step], spread_recv.at[step], lax.rem(me_p + step, n_psg), me_c,
        )
        copy.start()
        spread.append(copy)
        sent.append(copy)

    def forward(step, kind, which, to_c):
        place = gathered.at[block(lax.rem(me_p - step + n_psg, n_psg)), quarter(which)]
        copy = remote(
            place, place, pass_send.at[kind, step], pass_recv.at[kind, step], me_p, to_c
        )
        copy.start()
        sent.append(copy)
        return copy

    from_sibling, from_across = [], []
    for step in range(1, n_psg):
        spread[step].wait_recv()
        from_across.append(forward(step, 0, me_c, across))
        from_sibling.append(forward(step, 1, me_c, sibling))

    own.wait()
    tile = min(width, 256)

    def accumulate(at, arrivals):
        for copy in arrivals:
            copy.wait_recv()
        table_copies[at].wait()
        which = order[at]

        def multiply(number, carry):
            columns = pl.ds(pl.multiple_of(number * tile, tile), tile)
            product = lax.dot_general(
                gathered[:, quarter(which)], table[columns, quarter(which)],
                (((1,), (1,)), ((), ())), preferred_element_type=jnp.float32,
            )
            if at > 0:
                product = logits[:, columns] + product
            if at == len(order) - 1:
                product = product * factor
            logits[:, columns] = product
            return carry

        lax.fori_loop(0, width // tile, multiply, 0)

    accumulate(0, ())
    from_diagonal = []
    for step in range(1, n_psg):
        from_across[step - 1].wait_recv()
        from_diagonal.append(forward(step, 2, across, sibling))
    accumulate(1, from_sibling)
    accumulate(2, ())
    accumulate(3, from_diagonal)
    out_copy = pltpu.make_async_copy(gathered, gathered_out, out_sem)
    out_copy.start()

    chunks = width // LANES
    groups = 4 if chunks % 4 == 0 else 1

    slab = min(count, 32)

    def total_rows(number):
        def add(index, carry):
            rows = pl.ds(pl.multiple_of(index * slab, slab), slab)

            def shifted(chunk):
                place = slice(chunk * LANES, (chunk + 1) * LANES)
                return logits[rows, place] + cen_duals_ref[:, place]

            top = functools.reduce(jnp.maximum, [shifted(chunk) for chunk in range(chunks)])
            total = jnp.exp(shifted(0) - top)
            for chunk in range(1, chunks):
                total = total + jnp.exp(shifted(chunk) - top)
            lane_top[rows, :] = top
            lane_sum[rows, :] = total
            return carry

        lax.fori_loop(0, count // slab, add, 0, unroll=2)
        tops, sums = lane_top[...].T, lane_sum[...].T
        top = jnp.max(tops, axis=0, keepdims=True)
        total = jnp.sum(sums * jnp.exp(tops - top), axis=0, keepdims=True)
        top, total = exchange(
            number, top, total, cen_buf, cen_send, cen_recv, n_cen, me_c,
            lambda step: (me_p, lax.rem(me_c + step, n_cen)),
        )
        return exchange(
            number, top, total, psg_buf, psg_send, psg_recv, n_psg, me_p,
            lambda step: (lax.rem(me_p + step, n_psg), me_c),
        )

    def exchange(number, top, total, buf, send, recv, size, me, target):
        upper = lax.broadcasted_iota(jnp.int32, (8, count), 0) < 4
        buf[number, me] = jnp.where(upper, top, total)
        copies = []
        for step in range(1, size):
            to_p, to_c = target(step)
            copy = remote(
                buf.at[number, me], buf.at[number, me],
                send.at[number, step], recv.at[number, step], to_p, to_c,
            )
            copy.start()
            copies.append(copy)
            sent.append(copy)
        for copy in copies:
            copy.wait_recv()
        tops = [buf[number, other, 0:1, :] for other in range(size)]
        sums = [buf[number, other, 4:5, :] for other in range(size)]
        top = functools.reduce(jnp.maximum, tops)
        total = functools.reduce(
            jnp.add, [value * jnp.exp(high - top) for high, value in zip(tops, sums)]
        )
        return top, total

    cen_duals_ref[...] = init_ref[...]
    for number in range(ITERS):
        top, total = total_rows(number)
        duals = -math.log(count) - (top + jnp.log(total))
        duals_wide[...] = jnp.broadcast_to(duals, (LANES, count)).T
        last = number == ITERS - 1
        if last:
            duals_ref[...] = duals

        def columns_pass(index, carry, last=last):
            places = [lanes(index * groups + group) for group in range(groups)]
            terms = [logits[:, place] + duals_wide[...] for place in places]
            tops = [jnp.max(term, axis=0, keepdims=True) for term in terms]
            sums = [
                jnp.sum(jnp.exp(term - high), axis=0, keepdims=True)
                for term, high in zip(terms, tops)
            ]
            for place, term, high, value in zip(places, terms, tops, sums):
                fresh = -math.log(CENTROIDS) - (high + jnp.log(value))
                cen_duals_ref[:, place] = fresh
                if last:
                    weight_ref[:, place] = (CENTROIDS * jnp.exp(term + fresh)).astype(
                        jnp.bfloat16
                    )
            return carry

        lax.fori_loop(0, chunks // groups, columns_pass, 0)

    for copy in sent:
        copy.wait_send()
    out_copy.wait()


def update_kernel(n_psg, weight_ref, gathered_ref, duals_ref, cen_ref, out_ref, own_ref, cen_out_ref):
    depth = out_ref.shape[1]
    local = own_ref.shape[1]
    step = min(depth, 512)

    @pl.when(pl.program_id(0) == 0)
    def _():
        me = lax.axis_index("psg")
        own = duals_ref[:, 0:local]
        for index in range(1, n_psg):
            own = jnp.where(me == index, duals_ref[:, index * local:(index + 1) * local], own)
        own_ref[...] = own
        cen_out_ref[...] = cen_ref[...]

    weight = weight_ref[...].T
    for start in range(0, depth, step):
        out_ref[:, start:start + step] = lax.dot_general(
            weight, gathered_ref[:, start:start + step], (((1,), (0,)), ((), ())),
            preferred_element_type=jnp.float32,
        ).astype(out_ref.dtype)


def body(n_psg, n_cen, passages, centroids, dual_init):
    local, depth = passages.shape
    width = centroids.shape[0]
    count = local * n_psg
    vmem = pl.BlockSpec(memory_space=pltpu.VMEM)
    anywhere = pl.BlockSpec(memory_space=pl.ANY)
    dma = pltpu.SemaphoreType.DMA
    weight, gathered, passage_duals, centroid_duals = pl.pallas_call(
        functools.partial(kernel, n_psg, n_cen),
        out_shape=(
            jax.ShapeDtypeStruct((count, width), jnp.bfloat16),
            jax.ShapeDtypeStruct((count, depth), jnp.bfloat16),
            jax.ShapeDtypeStruct((1, count), jnp.float32),
            jax.ShapeDtypeStruct((1, width), jnp.float32),
        ),
        in_specs=[vmem, anywhere, vmem],
        out_specs=(vmem, anywhere, vmem, vmem),
        scratch_shapes=[
            pltpu.VMEM((width, depth), jnp.bfloat16),
            pltpu.VMEM((count, depth), jnp.bfloat16),
            pltpu.VMEM((count, width), jnp.float32),
            pltpu.VMEM((count, LANES), jnp.float32),
            pltpu.VMEM((count, LANES), jnp.float32),
            pltpu.VMEM((count, LANES), jnp.float32),
            pltpu.VMEM((ITERS, n_cen, 8, count), jnp.float32),
            pltpu.VMEM((ITERS, n_psg, 8, count), jnp.float32),
            dma((n_cen,)),
            dma,
            dma((n_psg,)),
            dma((n_psg,)),
            dma((3, n_psg)),
            dma((3, n_psg)),
            dma((ITERS, n_cen)),
            dma((ITERS, n_cen)),
            dma((ITERS, n_psg)),
            dma((ITERS, n_psg)),
            dma,
        ],
        compiler_params=pltpu.CompilerParams(
            collective_id=0, has_side_effects=True, vmem_limit_bytes=56 * 1024 * 1024
        ),
    )(passages, centroids, dual_init.reshape(1, width))
    tile = min(width, 512)
    new_centroids, own_duals, final_duals = pl.pallas_call(
        functools.partial(update_kernel, n_psg),
        grid=(width // tile,),
        out_shape=(
            jax.ShapeDtypeStruct((width, depth), jnp.bfloat16),
            jax.ShapeDtypeStruct((1, local), jnp.float32),
            jax.ShapeDtypeStruct((1, width), jnp.float32),
        ),
        in_specs=[
            pl.BlockSpec((count, tile), lambda i: (0, i)),
            pl.BlockSpec((count, depth), lambda i: (0, 0)),
            pl.BlockSpec((1, count), lambda i: (0, 0)),
            pl.BlockSpec((1, width), lambda i: (0, 0)),
        ],
        out_specs=(
            pl.BlockSpec((tile, depth), lambda i: (i, 0)),
            pl.BlockSpec((1, local), lambda i: (0, 0)),
            pl.BlockSpec((1, width), lambda i: (0, 0)),
        ),
        compiler_params=pltpu.CompilerParams(vmem_limit_bytes=60 * 1024 * 1024),
    )(weight, gathered, passage_duals, centroid_duals)
    return (new_centroids, own_duals.reshape(local), final_duals.reshape(width))


def solution(mesh):
    in_specs = (P("psg", None), P(("psg", "cen"), None), P(("psg", "cen")))
    out_specs = (P(("psg", "cen"), None), P("psg"), P(("psg", "cen")))
    return jax.shard_map(
        functools.partial(body, mesh.shape["psg"], mesh.shape["cen"]),
        mesh=mesh, in_specs=in_specs, out_specs=out_specs, check_vma=False,
    )
```

```python
import functools
import math

import jax
import jax.numpy as jnp
from jax import lax
from jax.experimental import pallas as pl
from jax.experimental.pallas import tpu as pltpu
from jax.sharding import PartitionSpec as P

CENTROIDS = 65536
ITERS = 3
LANES = 128
MESH = pl.DeviceIdType.MESH


def kernel(
    n_psg, n_cen,
    rows_ref, table_ref, init_ref,
    weight_ref, gathered_out, duals_ref, cen_duals_ref,
    table, gathered, logits, lane_top, lane_sum, duals_wide, cen_buf, psg_buf,
    table_sem, own_sem, pass_send, pass_recv,
    cen_send, cen_recv, psg_send, psg_recv, out_sem,
):
    me_p, me_c = lax.axis_index("psg"), lax.axis_index("cen")
    local, depth = rows_ref.shape
    count, width = logits.shape
    part = depth // n_cen
    factor = 4.0 / math.sqrt(depth)
    sibling = me_c + 1 - 2 * lax.rem(me_c, 2)
    across = lax.rem(me_c + 2, n_cen)
    diagonal = lax.rem(sibling + 2, n_cen)
    order = (me_c, sibling, across, diagonal)

    def block(index):
        return pl.ds(pl.multiple_of(index * local, local), local)

    def quarter(index):
        return pl.ds(pl.multiple_of(index * part, part), part)

    def lanes(index):
        return pl.ds(pl.multiple_of(index * LANES, LANES), LANES)

    table_copies = []
    for at, which in enumerate(order):
        copy = pltpu.make_async_copy(
            table_ref.at[:, quarter(which)], table.at[:, quarter(which)], table_sem.at[at]
        )
        copy.start()
        table_copies.append(copy)
    own = pltpu.make_async_copy(rows_ref, gathered.at[block(me_p), :], own_sem)
    own.start()

    barrier = pltpu.get_barrier_semaphore()
    for step in range(1, n_psg):
        pl.semaphore_signal(
            barrier, inc=1, device_id=(lax.rem(me_p + step, n_psg), me_c), device_id_type=MESH
        )
    for step in range(1, n_cen):
        pl.semaphore_signal(
            barrier, inc=1, device_id=(me_p, lax.rem(me_c + step, n_cen)), device_id_type=MESH
        )
    pl.semaphore_wait(barrier, n_psg + n_cen - 2)

    def remote(src, dst, send, recv, to_p, to_c):
        return pltpu.make_async_remote_copy(
            src_ref=src, dst_ref=dst, send_sem=send, recv_sem=recv,
            device_id=(to_p, to_c), device_id_type=MESH,
        )

    sent = []

    def send(kind, row, step, rows, columns, to_p, to_c, source=None):
        place = gathered.at[rows, columns]
        copy = remote(
            place if source is None else source, place,
            pass_send.at[kind, row, step], pass_recv.at[kind, row, step], to_p, to_c,
        )
        copy.start()
        sent.append(copy)
        return copy

    pairs = n_psg // 2
    me_z, me_x = me_p // 2, lax.rem(me_p, 2)
    mate = me_p + 1 - 2 * me_x

    def eighth(index, side):
        return pl.ds(pl.multiple_of(index * part + side * (part // 2), part // 2), part // 2)

    def pair(step):
        index = lax.rem(me_z - step + pairs, pairs)
        return pl.ds(pl.multiple_of(index * 2 * local, 2 * local), 2 * local)

    def peer(step):
        return lax.rem(me_z + step, pairs) * 2 + me_x

    mine = eighth(me_c, me_x)
    to_mate = [
        send(
            0, 0, 0, block(me_p), quarter(me_c), mate, me_c,
            source=rows_ref.at[:, quarter(me_c)],
        )
    ]
    along = [[None], [None]]
    for step in range(1, pairs):
        along[0].append(
            send(1, 0, step, block(me_p), mine, peer(step), me_c, source=rows_ref.at[:, mine])
        )
    to_mate[0].wait_recv()
    for step in range(1, pairs):
        along[1].append(send(1, 1, step, block(mate), mine, peer(step), me_c))
    pieces = [(0, 0, block(mate), None)]
    from_across = [send(2, 0, 0, block(mate), quarter(me_c), me_p, across)]
    from_sibling = [send(3, 0, 0, block(mate), quarter(me_c), me_p, sibling)]
    for row in range(2):
        side = me_x if row == 0 else 1 - me_x
        for step in range(1, pairs):
            if row == 0:
                along[0][step].wait_recv()
                along[1][step].wait_recv()
                to_mate.append(send(0, 0, step, pair(step), mine, mate, me_c))
            else:
                to_mate[step].wait_recv()
            pieces.append((row, step, pair(step), side))
            columns = eighth(me_c, side)
            from_across.append(send(2, row, step, pair(step), columns, me_p, across))
            from_sibling.append(send(3, row, step, pair(step), columns, me_p, sibling))

    own.wait()
    tile = min(width, 256)

    def accumulate(at, arrivals):
        for copy in arrivals:
            copy.wait_recv()
        table_copies[at].wait()
        which = order[at]

        def multiply(number, carry):
            columns = pl.ds(pl.multiple_of(number * tile, tile), tile)
            product = lax.dot_general(
                gathered[:, quarter(which)], table[columns, quarter(which)],
                (((1,), (1,)), ((), ())), preferred_element_type=jnp.float32,
            )
            if at > 0:
                product = logits[:, columns] + product
            if at == len(order) - 1:
                product = product * factor
            logits[:, columns] = product
            return carry

        lax.fori_loop(0, width // tile, multiply, 0)

    accumulate(0, ())
    accumulate(1, from_sibling)
    from_diagonal = []
    for copy, (row, step, rows, side) in zip(from_across, pieces):
        copy.wait_recv()
        columns = quarter(across) if side is None else eighth(across, side)
        from_diagonal.append(send(4, row, step, rows, columns, me_p, sibling))
    accumulate(2, ())
    accumulate(3, from_diagonal)
    out_copy = pltpu.make_async_copy(gathered, gathered_out, out_sem)
    out_copy.start()

    chunks = width // LANES
    groups = 4 if chunks % 4 == 0 else 1

    slab = min(count, 32)

    def total_rows(number):
        def add(index, carry):
            rows = pl.ds(pl.multiple_of(index * slab, slab), slab)

            def shifted(chunk):
                place = slice(chunk * LANES, (chunk + 1) * LANES)
                return logits[rows, place] + cen_duals_ref[:, place]

            top = functools.reduce(jnp.maximum, [shifted(chunk) for chunk in range(chunks)])
            total = jnp.exp(shifted(0) - top)
            for chunk in range(1, chunks):
                total = total + jnp.exp(shifted(chunk) - top)
            lane_top[rows, :] = top
            lane_sum[rows, :] = total
            return carry

        lax.fori_loop(0, count // slab, add, 0, unroll=2)
        tops, sums = lane_top[...].T, lane_sum[...].T
        top = jnp.max(tops, axis=0, keepdims=True)
        total = jnp.sum(sums * jnp.exp(tops - top), axis=0, keepdims=True)
        top, total = exchange(
            number, top, total, cen_buf, cen_send, cen_recv, n_cen, me_c,
            lambda step: (me_p, lax.rem(me_c + step, n_cen)),
        )
        return exchange(
            number, top, total, psg_buf, psg_send, psg_recv, n_psg, me_p,
            lambda step: (lax.rem(me_p + step, n_psg), me_c),
        )

    def exchange(number, top, total, buf, send, recv, size, me, target):
        upper = lax.broadcasted_iota(jnp.int32, (8, count), 0) < 4
        buf[number, me] = jnp.where(upper, top, total)
        copies = []
        for step in range(1, size):
            to_p, to_c = target(step)
            copy = remote(
                buf.at[number, me], buf.at[number, me],
                send.at[number, step], recv.at[number, step], to_p, to_c,
            )
            copy.start()
            copies.append(copy)
            sent.append(copy)
        for copy in copies:
            copy.wait_recv()
        tops = [buf[number, other, 0:1, :] for other in range(size)]
        sums = [buf[number, other, 4:5, :] for other in range(size)]
        top = functools.reduce(jnp.maximum, tops)
        total = functools.reduce(
            jnp.add, [value * jnp.exp(high - top) for high, value in zip(tops, sums)]
        )
        return top, total

    cen_duals_ref[...] = init_ref[...]
    for number in range(ITERS):
        top, total = total_rows(number)
        duals = -math.log(count) - (top + jnp.log(total))
        duals_wide[...] = jnp.broadcast_to(duals, (LANES, count)).T
        last = number == ITERS - 1
        if last:
            duals_ref[...] = duals

        def columns_pass(index, carry, last=last):
            places = [lanes(index * groups + group) for group in range(groups)]
            terms = [logits[:, place] + duals_wide[...] for place in places]
            tops = [jnp.max(term, axis=0, keepdims=True) for term in terms]
            sums = [
                jnp.sum(jnp.exp(term - high), axis=0, keepdims=True)
                for term, high in zip(terms, tops)
            ]
            for place, term, high, value in zip(places, terms, tops, sums):
                fresh = -math.log(CENTROIDS) - (high + jnp.log(value))
                cen_duals_ref[:, place] = fresh
                if last:
                    weight_ref[:, place] = (CENTROIDS * jnp.exp(term + fresh)).astype(
                        jnp.bfloat16
                    )
            return carry

        lax.fori_loop(0, chunks // groups, columns_pass, 0)

    for copy in sent:
        copy.wait_send()
    out_copy.wait()


def update_kernel(n_psg, weight_ref, gathered_ref, duals_ref, cen_ref, out_ref, own_ref, cen_out_ref):
    depth = out_ref.shape[1]
    local = own_ref.shape[1]
    step = min(depth, 512)

    @pl.when(pl.program_id(0) == 0)
    def _():
        me = lax.axis_index("psg")
        own = duals_ref[:, 0:local]
        for index in range(1, n_psg):
            own = jnp.where(me == index, duals_ref[:, index * local:(index + 1) * local], own)
        own_ref[...] = own
        cen_out_ref[...] = cen_ref[...]

    weight = weight_ref[...].T
    for start in range(0, depth, step):
        out_ref[:, start:start + step] = lax.dot_general(
            weight, gathered_ref[:, start:start + step], (((1,), (0,)), ((), ())),
            preferred_element_type=jnp.float32,
        ).astype(out_ref.dtype)


def body(n_psg, n_cen, passages, centroids, dual_init):
    local, depth = passages.shape
    width = centroids.shape[0]
    count = local * n_psg
    vmem = pl.BlockSpec(memory_space=pltpu.VMEM)
    anywhere = pl.BlockSpec(memory_space=pl.ANY)
    dma = pltpu.SemaphoreType.DMA
    weight, gathered, passage_duals, centroid_duals = pl.pallas_call(
        functools.partial(kernel, n_psg, n_cen),
        out_shape=(
            jax.ShapeDtypeStruct((count, width), jnp.bfloat16),
            jax.ShapeDtypeStruct((count, depth), jnp.bfloat16),
            jax.ShapeDtypeStruct((1, count), jnp.float32),
            jax.ShapeDtypeStruct((1, width), jnp.float32),
        ),
        in_specs=[vmem, anywhere, vmem],
        out_specs=(vmem, anywhere, vmem, vmem),
        scratch_shapes=[
            pltpu.VMEM((width, depth), jnp.bfloat16),
            pltpu.VMEM((count, depth), jnp.bfloat16),
            pltpu.VMEM((count, width), jnp.float32),
            pltpu.VMEM((count, LANES), jnp.float32),
            pltpu.VMEM((count, LANES), jnp.float32),
            pltpu.VMEM((count, LANES), jnp.float32),
            pltpu.VMEM((ITERS, n_cen, 8, count), jnp.float32),
            pltpu.VMEM((ITERS, n_psg, 8, count), jnp.float32),
            dma((n_cen,)),
            dma,
            dma((5, 2, n_psg // 2)),
            dma((5, 2, n_psg // 2)),
            dma((ITERS, n_cen)),
            dma((ITERS, n_cen)),
            dma((ITERS, n_psg)),
            dma((ITERS, n_psg)),
            dma,
        ],
        compiler_params=pltpu.CompilerParams(
            collective_id=0, has_side_effects=True, vmem_limit_bytes=56 * 1024 * 1024
        ),
    )(passages, centroids, dual_init.reshape(1, width))
    tile = min(width, 512)
    new_centroids, own_duals, final_duals = pl.pallas_call(
        functools.partial(update_kernel, n_psg),
        grid=(width // tile,),
        out_shape=(
            jax.ShapeDtypeStruct((width, depth), jnp.bfloat16),
            jax.ShapeDtypeStruct((1, local), jnp.float32),
            jax.ShapeDtypeStruct((1, width), jnp.float32),
        ),
        in_specs=[
            pl.BlockSpec((count, tile), lambda i: (0, i)),
            pl.BlockSpec((count, depth), lambda i: (0, 0)),
            pl.BlockSpec((1, count), lambda i: (0, 0)),
            pl.BlockSpec((1, width), lambda i: (0, 0)),
        ],
        out_specs=(
            pl.BlockSpec((tile, depth), lambda i: (i, 0)),
            pl.BlockSpec((1, local), lambda i: (0, 0)),
            pl.BlockSpec((1, width), lambda i: (0, 0)),
        ),
        compiler_params=pltpu.CompilerParams(vmem_limit_bytes=60 * 1024 * 1024),
    )(weight, gathered, passage_duals, centroid_duals)
    return (new_centroids, own_duals.reshape(local), final_duals.reshape(width))


def solution(mesh):
    in_specs = (P("psg", None), P(("psg", "cen"), None), P(("psg", "cen")))
    out_specs = (P(("psg", "cen"), None), P("psg"), P(("psg", "cen")))
    return jax.shard_map(
        functools.partial(body, mesh.shape["psg"], mesh.shape["cen"]),
        mesh=mesh, in_specs=in_specs, out_specs=out_specs, check_vma=False,
    )
```

```python
import functools
import math

import jax
import jax.numpy as jnp
from jax import lax
from jax.experimental import pallas as pl
from jax.experimental.pallas import tpu as pltpu
from jax.sharding import PartitionSpec as P

CENTROIDS = 65536
ITERS = 3
LANES = 128
MESH = pl.DeviceIdType.MESH


def kernel(
    n_psg, n_cen,
    rows_ref, table_ref, init_ref,
    weight_ref, gathered_out, duals_ref, cen_duals_ref,
    table, gathered, logits, lane_top, lane_sum, duals_wide, cen_buf, psg_buf,
    table_sem, own_sem, pass_send, pass_recv,
    cen_send, cen_recv, psg_send, psg_recv, out_sem,
):
    me_p, me_c = lax.axis_index("psg"), lax.axis_index("cen")
    local, depth = rows_ref.shape
    count, width = logits.shape
    part = depth // n_cen
    factor = 4.0 / math.sqrt(depth)
    sibling = me_c + 1 - 2 * lax.rem(me_c, 2)
    across = lax.rem(me_c + 2, n_cen)
    diagonal = lax.rem(sibling + 2, n_cen)
    order = (me_c, sibling, across, diagonal)

    def block(index):
        return pl.ds(pl.multiple_of(index * local, local), local)

    def quarter(index):
        return pl.ds(pl.multiple_of(index * part, part), part)

    def lanes(index):
        return pl.ds(pl.multiple_of(index * LANES, LANES), LANES)

    table_copies = []
    for at, which in enumerate(order):
        copy = pltpu.make_async_copy(
            table_ref.at[:, quarter(which)], table.at[:, quarter(which)], table_sem.at[at]
        )
        copy.start()
        table_copies.append(copy)
    own = pltpu.make_async_copy(rows_ref, gathered.at[block(me_p), :], own_sem)
    own.start()

    barrier = pltpu.get_barrier_semaphore()
    for step in range(1, n_psg):
        pl.semaphore_signal(
            barrier, inc=1, device_id=(lax.rem(me_p + step, n_psg), me_c), device_id_type=MESH
        )
    for step in range(1, n_cen):
        pl.semaphore_signal(
            barrier, inc=1, device_id=(me_p, lax.rem(me_c + step, n_cen)), device_id_type=MESH
        )
    pl.semaphore_wait(barrier, n_psg + n_cen - 2)

    def remote(src, dst, send, recv, to_p, to_c):
        return pltpu.make_async_remote_copy(
            src_ref=src, dst_ref=dst, send_sem=send, recv_sem=recv,
            device_id=(to_p, to_c), device_id_type=MESH,
        )

    sent = []

    def send(kind, row, step, rows, columns, to_p, to_c, source=None):
        place = gathered.at[rows, columns]
        copy = remote(
            place if source is None else source, place,
            pass_send.at[kind, row, step], pass_recv.at[kind, row, step], to_p, to_c,
        )
        copy.start()
        sent.append(copy)
        return copy

    pairs = n_psg // 2
    me_z, me_x = me_p // 2, lax.rem(me_p, 2)
    mate = me_p + 1 - 2 * me_x

    def eighth(index, side):
        return pl.ds(pl.multiple_of(index * part + side * (part // 2), part // 2), part // 2)

    def pair(step):
        index = lax.rem(me_z - step + pairs, pairs)
        return pl.ds(pl.multiple_of(index * 2 * local, 2 * local), 2 * local)

    def peer(step):
        return lax.rem(me_z + step, pairs) * 2 + me_x

    mine = eighth(me_c, me_x)
    to_mate = [
        send(
            0, 0, 0, block(me_p), quarter(me_c), mate, me_c,
            source=rows_ref.at[:, quarter(me_c)],
        )
    ]
    along = [[None], [None]]
    for step in range(1, pairs):
        along[0].append(
            send(1, 0, step, block(me_p), mine, peer(step), me_c, source=rows_ref.at[:, mine])
        )
    to_mate[0].wait_recv()
    for step in range(1, pairs):
        along[1].append(send(1, 1, step, block(mate), mine, peer(step), me_c))
    pieces = [(0, 0, block(mate), None)]
    from_across = [send(2, 0, 0, block(mate), quarter(me_c), me_p, across)]
    from_sibling = [send(3, 0, 0, block(mate), quarter(me_c), me_p, sibling)]
    for row in range(2):
        side = me_x if row == 0 else 1 - me_x
        for step in range(1, pairs):
            if row == 0:
                along[0][step].wait_recv()
                along[1][step].wait_recv()
                to_mate.append(send(0, 0, step, pair(step), mine, mate, me_c))
            else:
                to_mate[step].wait_recv()
            pieces.append((row, step, pair(step), side))
            columns = eighth(me_c, side)
            from_across.append(send(2, row, step, pair(step), columns, me_p, across))
            from_sibling.append(send(3, row, step, pair(step), columns, me_p, sibling))

    own.wait()
    tile = min(width, 1024)

    def accumulate(at, arrivals):
        for copy in arrivals:
            copy.wait_recv()
        table_copies[at].wait()
        which = order[at]

        def multiply(number, carry):
            columns = pl.ds(pl.multiple_of(number * tile, tile), tile)
            product = lax.dot_general(
                gathered[:, quarter(which)], table[columns, quarter(which)],
                (((1,), (1,)), ((), ())), preferred_element_type=jnp.float32,
            )
            if at > 0:
                product = logits[:, columns] + product
            if at == len(order) - 1:
                product = product * factor
            logits[:, columns] = product
            return carry

        lax.fori_loop(0, width // tile, multiply, 0)

    accumulate(0, ())
    accumulate(1, from_sibling)
    from_diagonal = []
    for copy, (row, step, rows, side) in zip(from_across, pieces):
        copy.wait_recv()
        columns = quarter(across) if side is None else eighth(across, side)
        from_diagonal.append(send(4, row, step, rows, columns, me_p, sibling))
    accumulate(2, ())
    accumulate(3, from_diagonal)
    out_copy = pltpu.make_async_copy(gathered, gathered_out, out_sem)
    out_copy.start()

    chunks = width // LANES
    groups = 4 if chunks % 4 == 0 else 1

    slab = min(count, 32)

    def total_rows(number):
        def add(index, carry):
            rows = pl.ds(pl.multiple_of(index * slab, slab), slab)

            def shifted(chunk):
                place = slice(chunk * LANES, (chunk + 1) * LANES)
                return logits[rows, place] + cen_duals_ref[:, place]

            top = functools.reduce(jnp.maximum, [shifted(chunk) for chunk in range(chunks)])
            total = jnp.exp(shifted(0) - top)
            for chunk in range(1, chunks):
                total = total + jnp.exp(shifted(chunk) - top)
            lane_top[rows, :] = top
            lane_sum[rows, :] = total
            return carry

        lax.fori_loop(0, count // slab, add, 0, unroll=2)
        tops, sums = lane_top[...].T, lane_sum[...].T
        top = jnp.max(tops, axis=0, keepdims=True)
        total = jnp.sum(sums * jnp.exp(tops - top), axis=0, keepdims=True)
        top, total = exchange(
            number, top, total, cen_buf, cen_send, cen_recv, n_cen, me_c,
            lambda step: (me_p, lax.rem(me_c + step, n_cen)),
        )
        return exchange(
            number, top, total, psg_buf, psg_send, psg_recv, n_psg, me_p,
            lambda step: (lax.rem(me_p + step, n_psg), me_c),
        )

    def exchange(number, top, total, buf, send, recv, size, me, target):
        upper = lax.broadcasted_iota(jnp.int32, (8, count), 0) < 4
        buf[number, me] = jnp.where(upper, top, total)
        copies = []
        for step in range(1, size):
            to_p, to_c = target(step)
            copy = remote(
                buf.at[number, me], buf.at[number, me],
                send.at[number, step], recv.at[number, step], to_p, to_c,
            )
            copy.start()
            copies.append(copy)
            sent.append(copy)
        for copy in copies:
            copy.wait_recv()
        tops = [buf[number, other, 0:1, :] for other in range(size)]
        sums = [buf[number, other, 4:5, :] for other in range(size)]
        top = functools.reduce(jnp.maximum, tops)
        total = functools.reduce(
            jnp.add, [value * jnp.exp(high - top) for high, value in zip(tops, sums)]
        )
        return top, total

    cen_duals_ref[...] = init_ref[...]
    for number in range(ITERS):
        top, total = total_rows(number)
        duals = -math.log(count) - (top + jnp.log(total))
        duals_wide[...] = jnp.broadcast_to(duals, (LANES, count)).T
        last = number == ITERS - 1
        if last:
            duals_ref[...] = duals

        def columns_pass(index, carry, last=last):
            places = [lanes(index * groups + group) for group in range(groups)]
            terms = [logits[:, place] + duals_wide[...] for place in places]
            tops = [jnp.max(term, axis=0, keepdims=True) for term in terms]
            sums = [
                jnp.sum(jnp.exp(term - high), axis=0, keepdims=True)
                for term, high in zip(terms, tops)
            ]
            for place, term, high, value in zip(places, terms, tops, sums):
                fresh = -math.log(CENTROIDS) - (high + jnp.log(value))
                cen_duals_ref[:, place] = fresh
                if last:
                    weight_ref[:, place] = (CENTROIDS * jnp.exp(term + fresh)).astype(
                        jnp.bfloat16
                    )
            return carry

        lax.fori_loop(0, chunks // groups, columns_pass, 0)

    for copy in sent:
        copy.wait_send()
    out_copy.wait()


def update_kernel(n_psg, weight_ref, gathered_ref, duals_ref, cen_ref, out_ref, own_ref, cen_out_ref):
    depth = out_ref.shape[1]
    local = own_ref.shape[1]
    step = min(depth, 512)

    @pl.when(pl.program_id(0) == 0)
    def _():
        me = lax.axis_index("psg")
        own = duals_ref[:, 0:local]
        for index in range(1, n_psg):
            own = jnp.where(me == index, duals_ref[:, index * local:(index + 1) * local], own)
        own_ref[...] = own
        cen_out_ref[...] = cen_ref[...]

    weight = weight_ref[...].T
    for start in range(0, depth, step):
        out_ref[:, start:start + step] = lax.dot_general(
            weight, gathered_ref[:, start:start + step], (((1,), (0,)), ((), ())),
            preferred_element_type=jnp.float32,
        ).astype(out_ref.dtype)


def body(n_psg, n_cen, passages, centroids, dual_init):
    local, depth = passages.shape
    width = centroids.shape[0]
    count = local * n_psg
    vmem = pl.BlockSpec(memory_space=pltpu.VMEM)
    anywhere = pl.BlockSpec(memory_space=pl.ANY)
    dma = pltpu.SemaphoreType.DMA
    weight, gathered, passage_duals, centroid_duals = pl.pallas_call(
        functools.partial(kernel, n_psg, n_cen),
        out_shape=(
            jax.ShapeDtypeStruct((count, width), jnp.bfloat16),
            jax.ShapeDtypeStruct((count, depth), jnp.bfloat16),
            jax.ShapeDtypeStruct((1, count), jnp.float32),
            jax.ShapeDtypeStruct((1, width), jnp.float32),
        ),
        in_specs=[vmem, anywhere, vmem],
        out_specs=(vmem, anywhere, vmem, vmem),
        scratch_shapes=[
            pltpu.VMEM((width, depth), jnp.bfloat16),
            pltpu.VMEM((count, depth), jnp.bfloat16),
            pltpu.VMEM((count, width), jnp.float32),
            pltpu.VMEM((count, LANES), jnp.float32),
            pltpu.VMEM((count, LANES), jnp.float32),
            pltpu.VMEM((count, LANES), jnp.float32),
            pltpu.VMEM((ITERS, n_cen, 8, count), jnp.float32),
            pltpu.VMEM((ITERS, n_psg, 8, count), jnp.float32),
            dma((n_cen,)),
            dma,
            dma((5, 2, n_psg // 2)),
            dma((5, 2, n_psg // 2)),
            dma((ITERS, n_cen)),
            dma((ITERS, n_cen)),
            dma((ITERS, n_psg)),
            dma((ITERS, n_psg)),
            dma,
        ],
        compiler_params=pltpu.CompilerParams(
            collective_id=0, has_side_effects=True, vmem_limit_bytes=56 * 1024 * 1024
        ),
    )(passages, centroids, dual_init.reshape(1, width))
    tile = min(width, 512)
    new_centroids, own_duals, final_duals = pl.pallas_call(
        functools.partial(update_kernel, n_psg),
        grid=(width // tile,),
        out_shape=(
            jax.ShapeDtypeStruct((width, depth), jnp.bfloat16),
            jax.ShapeDtypeStruct((1, local), jnp.float32),
            jax.ShapeDtypeStruct((1, width), jnp.float32),
        ),
        in_specs=[
            pl.BlockSpec((count, tile), lambda i: (0, i)),
            pl.BlockSpec((count, depth), lambda i: (0, 0)),
            pl.BlockSpec((1, count), lambda i: (0, 0)),
            pl.BlockSpec((1, width), lambda i: (0, 0)),
        ],
        out_specs=(
            pl.BlockSpec((tile, depth), lambda i: (i, 0)),
            pl.BlockSpec((1, local), lambda i: (0, 0)),
            pl.BlockSpec((1, width), lambda i: (0, 0)),
        ),
        compiler_params=pltpu.CompilerParams(vmem_limit_bytes=60 * 1024 * 1024),
    )(weight, gathered, passage_duals, centroid_duals)
    return (new_centroids, own_duals.reshape(local), final_duals.reshape(width))


def solution(mesh):
    in_specs = (P("psg", None), P(("psg", "cen"), None), P(("psg", "cen")))
    out_specs = (P(("psg", "cen"), None), P("psg"), P(("psg", "cen")))
    return jax.shard_map(
        functools.partial(body, mesh.shape["psg"], mesh.shape["cen"]),
        mesh=mesh, in_specs=in_specs, out_specs=out_specs, check_vma=False,
    )
```
